32 devices in a mesh: seg: 16 (over z, y, x), samp: 2 (over core).
Axes of the slice: x: 2, y: 2, z: 4, core: 2. Of those that a mesh axis runs over, the one named last changes fastest.
Arguments:
- rigidity_diagonal_cells: bfloat16 [512, 128, 128], P('seg')
- rigidity_lower_cells: bfloat16 [512, 128, 128], P('seg'), may hold values from -0.5 to 0.5
- inverse_diagonal_cells: bfloat16 [512, 128, 128], P('seg')
- bedding_rigidity_per_unknown: float32 [512, 128], P('seg'), may hold values from 0.3 to 2
- bedding_regime: int32 [512], P('seg'), may hold values from 0 to 2
- dilation_push_per_kelvin: float32 [512, 128], P('seg'), may hold values from 1 to 16
- heat_shape_functions: bfloat16 [512, 512], P('seg'), may hold values from -0.25 to 0.25
- sampled_shape_weights: bfloat16 [64, 512], P('samp'), may hold values from -6 to 6
- joined_segment_table: int32 [16, 2], P('seg'), may hold values from 0 to 15
- joint_rigidity: float32 [16, 2], P('seg'), may hold values from 1.2 to 3.6
Outputs:
- displacement: float32 [64, 512, 128], P('samp', 'seg')
- kl_grad: float32 [512], replicated
The draws below stay inside these ranges and needn't reach their ends.
Inputs may be any that keep to these rules, and one draw needn't show every extreme that they name: `joined_segment_table`: every entry names a segment.
All inputs are finite; a program needn't handle non-finite values.
Results may differ from the reference program's by a relative error of at most 0.013.
Values may be sent and summed in bfloat16 or wider, within the bound.
A program may use at most 64 MiB of HBM per device.

```python
import math
import jax
import jax.numpy as jnp
from jax import lax

B = 128
EXPANSION_TERMS = 512
NB = 32
STEPS = 4
NLINK = 2
SEGS = 16
TRACK_PIECES = 512
SAMPLES = 64


def joint_rows_mask():
    return (jnp.arange(TRACK_PIECES) % NB == 0)[:, None]


def joint_values(key):
    inner_key = jax.random.fold_in(key, 31)
    exponent = jax.random.uniform(inner_key, (SEGS, NLINK), jnp.float32, math.log(1.2), math.log(3.6))
    return jnp.exp(exponent)


def diagonal_values(key):
    key_diag = jax.random.fold_in(key, 11)
    base_values = jax.random.uniform(key_diag, (TRACK_PIECES, B), jnp.float32, 4.0, 7.0)
    return base_values + 1.5 * joint_rows_mask().astype(jnp.float32)


def draw_rigidity_diagonal_cells(key, part):
    key_noise = jax.random.fold_in(key, 12)
    diagonal = diagonal_values(key)
    noise = jax.random.normal(key_noise, (TRACK_PIECES, B, B), jnp.float32) / math.sqrt(B)
    identity = jnp.eye(B, dtype=jnp.float32)
    return (noise + identity[None] * diagonal[:, None, :]).astype(jnp.bfloat16)


def draw_inverse_diagonal_cells(key, part):
    key_diag = jax.random.fold_in(key, 21)
    key_noise = jax.random.fold_in(key, 22)
    key_ratio = jax.random.fold_in(key, 23)
    interior = jax.random.uniform(key_diag, (TRACK_PIECES, B), jnp.float32, 0.08, 0.12)
    noise = jax.random.normal(key_noise, (TRACK_PIECES, B, B), jnp.float32) * (0.03 / math.sqrt(B))
    ratio = jax.random.uniform(key_ratio, (TRACK_PIECES, B), jnp.float32, 1.45, 1.7)
    joint_sum = jnp.sum(joint_values(key), axis=1)
    joint_rows_sum = jnp.repeat(joint_sum, NB)[:, None]
    joined_value = ratio / (diagonal_values(key) + joint_rows_sum + 1.0)
    diagonal = jnp.where(joint_rows_mask(), joined_value, interior)
    identity = jnp.eye(B, dtype=jnp.float32)
    return (noise + identity[None] * diagonal[:, None, :]).astype(jnp.bfloat16)


def draw_joint_rigidity(key, part):
    return joint_values(key)


def draw_dilation_push_per_kelvin(key, part):
    key_inner = jax.random.fold_in(key, 41)
    key_joint = jax.random.fold_in(key, 42)
    inner_values = jnp.exp(jax.random.uniform(key_inner, (TRACK_PIECES, B), jnp.float32, 0.0, math.log(4.0)))
    joint_push = jnp.exp(jax.random.uniform(key_joint, (TRACK_PIECES, B), jnp.float32, math.log(6.0), math.log(16.0)))
    return jnp.where(joint_rows_mask(), joint_push, inner_values)


def set_ends(drawn, key, low, high):
    longest = drawn.shape.index(max(drawn.shape))
    spots = []
    for shift in (0, 1):
        where = [jax.random.randint(jax.random.fold_in(key, axis), (), 0, length) for axis, length in enumerate(drawn.shape)]
        where[longest] = (where[longest] + shift) % drawn.shape[longest]
        spots.append(tuple(where))
    return drawn.at[spots[0]].set(low).at[spots[1]].set(high)


def steps_of(key, dims, cuts, least, largest):
    def one(position, blocks):
        draws = jax.random.uniform(jax.random.fold_in(jax.random.fold_in(key, 6), position), (blocks,), jnp.float32, least / len(cuts), largest / len(cuts))
        return jnp.repeat(jnp.exp(draws), dims[position] // blocks).reshape((-1,) + (1,) * (len(dims) - position - 1))

    level = one(*cuts[0])
    for cut in cuts[1:]:
        level = level * one(*cut)
    return level


def gaussian(stream_key, extent, spread, bound, cuts=(), kind=jnp.bfloat16):
    gain = steps_of(stream_key, extent, cuts, -0.22, 0.18) if cuts else 1.0
    values = jax.random.normal(stream_key, extent, jnp.float32) * spread * gain
    return jnp.minimum(jnp.maximum(values, -bound), bound).astype(kind)


def setup_inputs(seed: int = 0) -> dict:
    splits = jax.random.split(jax.random.key(seed), 11)
    return {
        "rigidity_diagonal_cells": draw_rigidity_diagonal_cells(jax.random.fold_in(splits[10], 71), 0),
        "rigidity_lower_cells": gaussian(splits[1], (TRACK_PIECES, B, B), B ** -0.5, 0.5, ((0, 16),)),
        "inverse_diagonal_cells": draw_inverse_diagonal_cells(jax.random.fold_in(splits[10], 71), 0),
        "bedding_rigidity_per_unknown": jnp.clip(jnp.exp(math.log(2.0) - 1.89712 * jax.random.uniform(splits[3], (TRACK_PIECES, B), jnp.float32) ** steps_of(splits[3], (TRACK_PIECES, B), ((0, 16),), -0.2, 0.2)), 0.3, 2.0),
        "bedding_regime": set_ends(jax.random.randint(splits[4], (TRACK_PIECES,), 0, 3), jax.random.fold_in(splits[4], 1), 0, 2).astype(jnp.int32),
        "dilation_push_per_kelvin": draw_dilation_push_per_kelvin(jax.random.fold_in(splits[10], 71), 0),
        "heat_shape_functions": gaussian(splits[6], (TRACK_PIECES, EXPANSION_TERMS), EXPANSION_TERMS ** -0.5, 0.25, ((0, 16),)),
        "sampled_shape_weights": gaussian(splits[7], (SAMPLES, EXPANSION_TERMS), 1.0, 6.0, ((0, 2),)),
        "joined_segment_table": set_ends(jax.random.randint(splits[8], (SEGS, NLINK), 0, SEGS), jax.random.fold_in(splits[8], 1), 0, SEGS - 1).astype(jnp.int32),
        "joint_rigidity": draw_joint_rigidity(jax.random.fold_in(splits[10], 71), 0),
    }


def stiffness(field_round, diag_full, couple_full, joined_segment_table, joint_rigidity):
    field = field_round.astype(jnp.float32)
    samples = field.shape[0]
    own_term = jnp.einsum('sjb,jab->sja', field, diag_full)
    upward = jnp.einsum('sjb,jba->sja', field, couple_full)
    upward = lax.optimization_barrier(upward.astype(jnp.bfloat16)).astype(jnp.float32)
    zero_block = jnp.zeros((samples, 1, B), jnp.float32)
    lower_field = jnp.concatenate([zero_block, field[:, :-1]], axis=1)
    below_term = jnp.einsum('sjb,jab->sja', lower_field, couple_full)
    upper_term = jnp.concatenate([upward[:, 1:], zero_block], axis=1)
    result = own_term + below_term + upper_term
    interfaces = field.reshape(samples, SEGS, NB, B)[:, :, 0, :]
    partner = interfaces[:, joined_segment_table, :]
    spring = lax.optimization_barrier(jnp.sum(joint_rigidity[None, :, :, None] * (interfaces[:, :, None, :] - partner), axis=2))
    result = result.reshape(samples, SEGS, NB, B).at[:, :, 0, :].add(spring)
    return result.reshape(samples, TRACK_PIECES, B)

def ballast(state, bedding_rigidity_per_unknown, bedding_regime):
    code = bedding_regime[None, :, None]
    stiff = bedding_rigidity_per_unknown[None]
    magnitude = 1.0 + jnp.abs(state)
    slide = jnp.tanh(state)
    force = jnp.where(code == 0, stiff * state, jnp.where(code == 1, stiff * state / magnitude, stiff * slide))
    tangent = jnp.where(code == 0, stiff + 0.0 * state, jnp.where(code == 1, stiff / (magnitude * magnitude), stiff * (1.0 - slide * slide)))
    return (force, tangent)

def blockwise(matrix_full, field_round):
    return jnp.einsum('jab,sjb->sja', matrix_full, field_round.astype(jnp.float32))

def reference(rigidity_diagonal_cells, rigidity_lower_cells, inverse_diagonal_cells, bedding_rigidity_per_unknown, bedding_regime, dilation_push_per_kelvin, heat_shape_functions, sampled_shape_weights, joined_segment_table, joint_rigidity):
    diag_full = rigidity_diagonal_cells.astype(jnp.float32)
    couple_full = rigidity_lower_cells.astype(jnp.float32)
    precond_full = inverse_diagonal_cells.astype(jnp.float32)
    complete_shape_functions = heat_shape_functions.astype(jnp.float32)
    heat_distribution = jnp.dot(sampled_shape_weights, heat_shape_functions.T, preferred_element_type=jnp.float32)
    heat_driven_source = dilation_push_per_kelvin[None] * heat_distribution[:, :, None]
    state = jnp.zeros((SAMPLES, TRACK_PIECES, B), jnp.float32)
    grad_total = jnp.zeros((EXPANSION_TERMS,), jnp.float32)
    for iteration in range(STEPS):
        state_round = state.astype(jnp.bfloat16)
        force, tangent = ballast(state, bedding_rigidity_per_unknown, bedding_regime)
        residual_vector = heat_driven_source - stiffness(state_round, diag_full, couple_full, joined_segment_table, joint_rigidity) - force
        initial_newton_step = blockwise(precond_full, residual_vector.astype(jnp.bfloat16))
        second = residual_vector - stiffness(initial_newton_step.astype(jnp.bfloat16), diag_full, couple_full, joined_segment_table, joint_rigidity) - tangent * initial_newton_step
        state = state + initial_newton_step + blockwise(precond_full, second.astype(jnp.bfloat16))
        next_round = state.astype(jnp.bfloat16).astype(jnp.float32)
        adjoint = jnp.einsum('sja,jab->sjb', next_round, precond_full)
        weighted = lax.optimization_barrier(jnp.sum(lax.optimization_barrier(jnp.sum(dilation_push_per_kelvin[None] * adjoint, axis=2)), axis=0))
        grad_total = grad_total + jnp.dot(weighted, complete_shape_functions, precision=lax.Precision.HIGHEST)
    scale = math.sqrt(EXPANSION_TERMS / (TRACK_PIECES * SAMPLES * B))
    return (state, grad_total * scale)
```

```python
import functools
import math

import jax
import jax.numpy as jnp
from jax import lax
from jax.experimental import pallas as pl
from jax.experimental.pallas import tpu as pltpu
from jax.sharding import PartitionSpec as P

STEPS = 4
EXCHANGES = 2 * STEPS - 1
GROUP = 6
F32 = jnp.float32
BF16 = jnp.bfloat16
MESH = pl.DeviceIdType.MESH


def dot_nt(left, right):
    return lax.dot_general(left, right, (((1,), (1,)), ((), ())), preferred_element_type=F32)


def dot_nn(left, right):
    return lax.dot_general(left, right, (((1,), (0,)), ((), ())), preferred_element_type=F32)


def kernel(
    segments,
    halves,
    diag_hbm,
    lower_hbm,
    inverse_hbm,
    bed_ref,
    regime_ref,
    push_ref,
    shape_ref,
    weight_ref,
    table_ref,
    joint_ref,
    x_ref,
    grad_ref,
    diag,
    lower,
    inverse,
    load,
    res,
    step_field,
    tangent,
    x_round,
    step_round,
    sample_sum,
    inverse_push,
    edge,
    below,
    partials,
    local_sem,
    send_sem,
    recv_sem,
    edge_send,
    edge_recv,
    cell_sem,
    sum_sem,
    *gathered,
):
    blocks = diag.shape[0]
    samples, width = load.shape[1], load.shape[2]
    me = lax.axis_index("seg")
    core = lax.axis_index("samp")
    devices = segments * halves
    flat = me * halves + core
    after = lax.rem(me + 1, segments)
    before = lax.rem(me + segments - 1, segments)

    barrier = pltpu.get_barrier_semaphore()

    def greet(k, carry):
        t = lax.rem(flat + k, devices)
        pl.semaphore_signal(
            barrier, inc=1, device_id=(t // halves, lax.rem(t, halves)), device_id_type=MESH
        )
        return carry

    lax.fori_loop(1, devices, greet, 0)

    loads = [
        pltpu.make_async_copy(inverse_hbm, inverse, local_sem.at[0]),
        pltpu.make_async_copy(diag_hbm, diag, local_sem.at[1]),
        pltpu.make_async_copy(lower_hbm, lower.at[pl.ds(0, blocks)], local_sem.at[2]),
    ]
    for copy in loads:
        copy.start()

    temperature = dot_nt(weight_ref[...], shape_ref[...])
    for j in range(blocks):
        load[j] = temperature[:, j : j + 1] * push_ref[j : j + 1, :]
    sample_sum[...] = jnp.zeros_like(sample_sum)

    def post(e, first_value, last_value):
        gathered[e][me] = first_value
        edge[e] = last_value

        def send(k, carry):
            pltpu.make_async_remote_copy(
                src_ref=gathered[e].at[me],
                dst_ref=gathered[e].at[me],
                send_sem=send_sem.at[e],
                recv_sem=recv_sem.at[e],
                device_id=(lax.rem(me + k, segments), core),
                device_id_type=MESH,
            ).start()
            return carry

        pltpu.make_async_remote_copy(
            src_ref=edge.at[e],
            dst_ref=below.at[e],
            send_sem=edge_send.at[e],
            recv_sem=edge_recv.at[e],
            device_id=(after, core),
            device_id_type=MESH,
        ).start()
        lax.fori_loop(1, segments, send, 0)

    def arrived(e):
        others = gathered[e].at[pl.ds(0, segments - 1)]
        pltpu.make_async_copy(others, others, recv_sem.at[e]).wait()
        pltpu.make_async_copy(below.at[e], below.at[e], edge_recv.at[e]).wait()

    def sent(e):
        others = gathered[e].at[pl.ds(0, segments - 1)]
        pltpu.make_async_copy(others, others, send_sem.at[e]).wait()
        pltpu.make_async_copy(edge.at[e], edge.at[e], edge_send.at[e]).wait()

    def stiff(low, own, high, j):
        pair = jnp.concatenate([low, own], axis=1)
        cells = jnp.concatenate([lower[j], diag[j]], axis=1)
        return dot_nt(pair, cells) + dot_nn(high, lower[j + 1])

    def spring(e, own):
        own = own.astype(F32)
        total = jnp.zeros_like(own)
        for l in range(table_ref.shape[1]):
            partner = gathered[e][table_ref[0, l]].astype(F32)
            total = total + joint_ref[0, l] * (own - partner)
        return total

    def ends(e, field):
        first_value, last_value = field[0], field[blocks - 1]
        low = stiff(below[e], first_value, field[1], 0) + spring(e, first_value)
        high = stiff(field[blocks - 2], last_value, gathered[e][after], blocks - 1)
        return low, high

    def ballast(x, j):
        k = bed_ref[pl.ds(j, 1), :]
        code = jnp.full(x.shape, regime_ref[j], jnp.int32)
        fraction = 1.0 / (1.0 + jnp.abs(x))
        slide = jnp.tanh(x)
        unit = jnp.where(code == 0, x, jnp.where(code == 1, x * fraction, slide))
        slope = jnp.where(
            code == 0, 1.0, jnp.where(code == 1, fraction * fraction, 1.0 - slide * slide)
        )
        return k * unit, k * slope

    def precondition(j, value):
        return dot_nt(value.astype(BF16), inverse[j])

    def finish_first(j, kx):
        force, slope = ballast(x_ref[j], j)
        residual = load[j] - kx - force
        first = precondition(j, residual)
        res[j] = residual
        tangent[j] = slope
        step_field[j] = first
        step_round[j] = first.astype(BF16)

    def finish_second(j, kf, start):
        first = step_field[j]
        if start:
            second = load[j] - kf - bed_ref[pl.ds(j, 1), :] * first
            x = first + precondition(j, second)
        else:
            second = res[j] - kf - tangent[j] * first
            x = x_ref[j] + first + precondition(j, second)
        rounded = x.astype(BF16)
        x_ref[j] = x
        x_round[j] = rounded
        sample_sum[pl.ds(j, 1), :] += jnp.sum(rounded.astype(F32), axis=0, keepdims=True)

    def every(start, stop, work):
        count = (stop - start) // GROUP

        def group(i, carry):
            for u in range(GROUP):
                work(start + i * GROUP + u)
            return carry

        lax.fori_loop(0, count, group, 0)
        for j in range(start + count * GROUP, stop):
            work(j)

    def start_first(j):
        first = precondition(j, load[j])
        step_field[j] = first
        step_round[j] = first.astype(BF16)

    loads[0].wait()
    start_first(0)
    start_first(blocks - 1)
    pl.semaphore_wait(barrier, devices - 1)
    post(0, step_round[0], step_round[blocks - 1])
    cell = pltpu.make_async_remote_copy(
        src_ref=lower_hbm.at[0],
        dst_ref=lower.at[blocks],
        send_sem=cell_sem.at[0],
        recv_sem=cell_sem.at[1],
        device_id=(before, core),
        device_id_type=MESH,
    )
    cell.start()
    every(1, blocks - 1, start_first)

    def push_product(j):
        push = push_ref[pl.ds(j, 1), :]
        high = push.astype(BF16)
        rest = push - high.astype(F32)
        middle = rest.astype(BF16)
        low = (rest - middle.astype(F32)).astype(BF16)
        rows = jnp.concatenate(
            [jnp.broadcast_to(part, (16, width)) for part in (high, middle, low)], axis=0
        )
        product = dot_nt(rows, inverse[j])
        inverse_push[pl.ds(j, 1), :] = product[0:1] + product[16:17] + product[32:33]

    every(0, blocks, push_product)
    loads[1].wait()
    loads[2].wait()

    def interior_first(j):
        finish_first(j, stiff(x_round[j - 1], x_round[j], x_round[j + 1], j))

    for step in range(STEPS):
        if step > 0:
            e = 2 * step - 1
            every(1, blocks - 1, interior_first)
            arrived(e)
            low, high = ends(e, x_round)
            finish_first(0, low)
            finish_first(blocks - 1, high)
            post(e + 1, step_round[0], step_round[blocks - 1])
        e = 2 * step

        def interior_second(j):
            kf = stiff(step_round[j - 1], step_round[j], step_round[j + 1], j)
            finish_second(j, kf, step == 0)

        every(1, blocks - 1, interior_second)
        arrived(e)
        if step == 0:
            cell.wait()
            lower[0] = jnp.where(jnp.full((width, width), me, jnp.int32) > 0, lower[0].astype(F32), 0.0).astype(BF16)
            lower[blocks] = jnp.where(
                jnp.full((width, width), me, jnp.int32) < segments - 1, lower[blocks].astype(F32), 0.0
            ).astype(BF16)
        low, high = ends(e, step_round)
        finish_second(0, low, step == 0)
        finish_second(blocks - 1, high, step == 0)
        if step < STEPS - 1:
            post(e + 1, x_round[0], x_round[blocks - 1])

    weighted = jnp.sum(inverse_push[...] * sample_sum[...], axis=1, keepdims=True)
    partials[flat] = jnp.sum(shape_ref[...].astype(F32) * weighted, axis=0, keepdims=True)

    def share(k, carry):
        t = lax.rem(flat + k, devices)
        pltpu.make_async_remote_copy(
            src_ref=partials.at[flat],
            dst_ref=partials.at[flat],
            send_sem=sum_sem.at[0],
            recv_sem=sum_sem.at[1],
            device_id=(t // halves, lax.rem(t, halves)),
            device_id_type=MESH,
        ).start()
        return carry

    lax.fori_loop(1, devices, share, 0)
    for e in range(EXCHANGES):
        sent(e)
    others = partials.at[pl.ds(0, devices - 1)]
    pltpu.make_async_copy(others, others, sum_sem.at[1]).wait()
    grad_ref[...] = jnp.sum(partials[...], axis=0)
    pltpu.make_async_copy(others, others, sum_sem.at[0]).wait()


def body(segments, halves, *arguments):
    (diag, lower, inverse, bed, regime, push, shapes, weights, table, joint) = arguments
    samples = weights.shape[0]
    blocks, width = diag.shape[0], diag.shape[1]
    terms = shapes.shape[1]
    devices = segments * halves
    vmem = pl.BlockSpec(memory_space=pltpu.VMEM)
    smem = pl.BlockSpec(memory_space=pltpu.SMEM)
    anywhere = pl.BlockSpec(memory_space=pltpu.HBM)
    field = (blocks, samples, width)
    rim = (EXCHANGES, samples, width)
    x, grad = pl.pallas_call(
        functools.partial(kernel, segments, halves),
        out_shape=(
            jax.ShapeDtypeStruct(field, F32),
            jax.ShapeDtypeStruct((1, terms), F32),
        ),
        in_specs=[anywhere, anywhere, anywhere, vmem, smem, vmem, vmem, vmem, smem, smem],
        out_specs=(vmem, vmem),
        scratch_shapes=[
            pltpu.VMEM((blocks, width, width), BF16),
            pltpu.VMEM((blocks + 1, width, width), BF16),
            pltpu.VMEM((blocks, width, width), BF16),
            pltpu.VMEM(field, F32),
            pltpu.VMEM(field, F32),
            pltpu.VMEM(field, F32),
            pltpu.VMEM(field, F32),
            pltpu.VMEM(field, BF16),
            pltpu.VMEM(field, BF16),
            pltpu.VMEM((blocks, width), F32),
            pltpu.VMEM((blocks, width), F32),
            pltpu.VMEM(rim, BF16),
            pltpu.VMEM(rim, BF16),
            pltpu.VMEM((devices, 1, terms), F32),
            pltpu.SemaphoreType.DMA((3,)),
            pltpu.SemaphoreType.DMA((EXCHANGES,)),
            pltpu.SemaphoreType.DMA((EXCHANGES,)),
            pltpu.SemaphoreType.DMA((EXCHANGES,)),
            pltpu.SemaphoreType.DMA((EXCHANGES,)),
            pltpu.SemaphoreType.DMA((2,)),
            pltpu.SemaphoreType.DMA((2,)),
        ]
        + [pltpu.VMEM((segments, samples, width), BF16)] * EXCHANGES,
        compiler_params=pltpu.CompilerParams(
            collective_id=0, has_side_effects=True, vmem_limit_bytes=40 * 1024 * 1024
        ),
    )(diag, lower, inverse, bed, regime, push, shapes, weights, table, joint)
    scale = math.sqrt(terms / (blocks * segments * samples * halves * width))
    return jnp.transpose(x, (1, 0, 2)), grad[0] * scale


def solution(mesh):
    placed = (
        P("seg", None, None),
        P("seg", None, None),
        P("seg", None, None),
        P("seg", None),
        P("seg"),
        P("seg", None),
        P("seg", None),
        P("samp", None),
        P("seg", None),
        P("seg", None),
    )
    return jax.shard_map(
        functools.partial(body, mesh.shape["seg"], mesh.shape["samp"]),
        mesh=mesh,
        in_specs=placed,
        out_specs=(P("samp", "seg", None), P()),
        check_vma=False,
    )
```

```python
import functools
import math

import jax
import jax.numpy as jnp
from jax import lax
from jax.experimental import pallas as pl
from jax.experimental.pallas import tpu as pltpu
from jax.sharding import PartitionSpec as P

STEPS = 4
EXCHANGES = 2 * STEPS - 1
GROUP = 10
F32 = jnp.float32
BF16 = jnp.bfloat16
MESH = pl.DeviceIdType.MESH


def dot_nt(left, right):
    return lax.dot_general(left, right, (((1,), (1,)), ((), ())), preferred_element_type=F32)


def dot_nn(left, right):
    return lax.dot_general(left, right, (((1,), (0,)), ((), ())), preferred_element_type=F32)


def kernel(
    segments,
    halves,
    diag_hbm,
    lower_hbm,
    inverse_hbm,
    bed_hbm,
    regime_ref,
    push_hbm,
    shape_hbm,
    weight_hbm,
    table_ref,
    joint_ref,
    x_hbm,
    grad_ref,
    diag,
    lower,
    inverse,
    bed_ref,
    push_ref,
    shape_ref,
    weight_ref,
    load,
    res,
    step_field,
    tangent,
    x_round,
    step_round,
    sample_sum,
    inverse_push,
    edge,
    below,
    partials,
    pair,
    x_ref,
    local_sem,
    send_sem,
    recv_sem,
    edge_send,
    edge_recv,
    cell_sem,
    sum_sem,
    *gathered,
):
    blocks = diag.shape[0]
    samples, width = load.shape[1], load.shape[2]
    me = lax.axis_index("seg")
    core = lax.axis_index("samp")
    after = lax.rem(me + 1, segments)
    before = lax.rem(me + segments - 1, segments)
    peers = segments + halves - 2

    barrier = pltpu.get_barrier_semaphore()

    def greet(k, carry):
        pl.semaphore_signal(
            barrier, inc=1, device_id=(lax.rem(me + k, segments), core), device_id_type=MESH
        )
        return carry

    def greet_half(k, carry):
        pl.semaphore_signal(
            barrier, inc=1, device_id=(me, lax.rem(core + k, halves)), device_id_type=MESH
        )
        return carry

    loads = [
        pltpu.make_async_copy(weight_hbm, weight_ref, local_sem.at[3]),
        pltpu.make_async_copy(shape_hbm, shape_ref, local_sem.at[4]),
        pltpu.make_async_copy(push_hbm, push_ref, local_sem.at[5]),
        pltpu.make_async_copy(bed_hbm, bed_ref, local_sem.at[6]),
        pltpu.make_async_copy(inverse_hbm, inverse, local_sem.at[0]),
        pltpu.make_async_copy(diag_hbm, diag, local_sem.at[1]),
        pltpu.make_async_copy(lower_hbm, lower.at[pl.ds(0, blocks)], local_sem.at[2]),
    ]
    for copy in loads:
        copy.start()
    lax.fori_loop(1, segments, greet, 0)
    lax.fori_loop(1, halves, greet_half, 0)
    for copy in loads[:4]:
        copy.wait()

    temperature = dot_nt(weight_ref[...], shape_ref[...])
    for j in range(blocks):
        load[j] = temperature[:, j : j + 1] * push_ref[j : j + 1, :]
    sample_sum[...] = jnp.zeros_like(sample_sum)

    def partner(k):
        return me ^ k if segments & (segments - 1) == 0 else lax.rem(me + k, segments)

    def post(e, first_value, last_value):
        gathered[e][me] = first_value
        edge[e] = last_value

        def send(k, carry):
            pltpu.make_async_remote_copy(
                src_ref=gathered[e].at[me],
                dst_ref=gathered[e].at[me],
                send_sem=send_sem.at[e],
                recv_sem=recv_sem.at[e],
                device_id=(partner(segments - k), core),
                device_id_type=MESH,
            ).start()
            return carry

        pltpu.make_async_remote_copy(
            src_ref=edge.at[e],
            dst_ref=below.at[e],
            send_sem=edge_send.at[e],
            recv_sem=edge_recv.at[e],
            device_id=(after, core),
            device_id_type=MESH,
        ).start()
        lax.fori_loop(1, segments, send, 0)

    def arrived(e):
        others = gathered[e].at[pl.ds(0, segments - 1)]
        pltpu.make_async_copy(others, others, recv_sem.at[e]).wait()
        pltpu.make_async_copy(below.at[e], below.at[e], edge_recv.at[e]).wait()

    def sent(e):
        others = gathered[e].at[pl.ds(0, segments - 1)]
        pltpu.make_async_copy(others, others, send_sem.at[e]).wait()
        pltpu.make_async_copy(edge.at[e], edge.at[e], edge_send.at[e]).wait()

    def stiff(low, own, high, j):
        pair = jnp.concatenate([low, own], axis=1)
        cells = jnp.concatenate([lower[j], diag[j]], axis=1)
        return dot_nt(pair, cells) + dot_nn(high, lower[j + 1])

    def spring(e, own):
        own = own.astype(F32)
        total = jnp.zeros_like(own)
        for l in range(table_ref.shape[1]):
            partner = gathered[e][table_ref[0, l]].astype(F32)
            total = total + joint_ref[0, l] * (own - partner)
        return total

    def ends_before(field):
        low = dot_nt(field[0], diag[0]) + dot_nn(field[1], lower[1])
        pair_cells = jnp.concatenate([lower[blocks - 1], diag[blocks - 1]], axis=1)
        high = dot_nt(jnp.concatenate([field[blocks - 2], field[blocks - 1]], axis=1), pair_cells)
        return low, high

    def ends_after(e, field, known):
        low = known[0] + dot_nt(below[e], lower[0]) + spring(e, field[0])
        high = known[1] + dot_nn(gathered[e][after], lower[blocks])
        return [low, high]

    def ballast(x, j):
        k = bed_ref[pl.ds(j, 1), :]
        code = jnp.full(x.shape, regime_ref[j], jnp.int32)
        fraction = 1.0 / (1.0 + jnp.abs(x))
        slide = jnp.tanh(x)
        unit = jnp.where(code == 0, x, jnp.where(code == 1, x * fraction, slide))
        slope = jnp.where(
            code == 0, 1.0, jnp.where(code == 1, fraction * fraction, 1.0 - slide * slide)
        )
        return k * unit, k * slope

    def precondition(j, value):
        return dot_nt(value.astype(BF16), inverse[j])

    def finish_first(js, kxs, pairs=None):
        if pairs is None:
            pairs = [ballast(x_ref[j], j) for j in js]
        residuals = [load[j] - kx - pair[0] for j, kx, pair in zip(js, kxs, pairs)]
        firsts = [precondition(j, residual) for j, residual in zip(js, residuals)]
        for j, residual, pair, first in zip(js, residuals, pairs, firsts):
            res[j] = residual
            tangent[j] = pair[1]
            step_field[j] = first
            step_round[j] = first.astype(BF16)

    def finish_second(js, kfs, start):
        firsts = [step_field[j] for j in js]
        if start:
            seconds = [
                load[j] - kf - bed_ref[pl.ds(j, 1), :] * first
                for j, kf, first in zip(js, kfs, firsts)
            ]
            xs = firsts
        else:
            seconds = [
                res[j] - kf - tangent[j] * first for j, kf, first in zip(js, kfs, firsts)
            ]
            xs = [x_ref[j] + first for j, first in zip(js, firsts)]
        xs = [x + precondition(j, second) for j, x, second in zip(js, xs, seconds)]
        rounds = [x.astype(BF16) for x in xs]
        sums = [jnp.sum(rounded.astype(F32), axis=0, keepdims=True) for rounded in rounds]
        for j, x, rounded, total in zip(js, xs, rounds, sums):
            x_ref[j] = x
            x_round[j] = rounded
            sample_sum[pl.ds(j, 1), :] += total

    def every(start, stop, work):
        count = (stop - start) // GROUP

        def group(i, carry):
            work([start + i * GROUP + u for u in range(GROUP)])
            return carry

        lax.fori_loop(0, count, group, 0)
        if start + count * GROUP < stop:
            work(list(range(start + count * GROUP, stop)))

    def start_first(js):
        firsts = [precondition(j, load[j]) for j in js]
        for j, first in zip(js, firsts):
            step_field[j] = first
            step_round[j] = first.astype(BF16)

    loads[4].wait()
    start_first([0, blocks - 1])
    pl.semaphore_wait(barrier, peers)
    post(0, step_round[0], step_round[blocks - 1])
    cell = pltpu.make_async_remote_copy(
        src_ref=lower_hbm.at[0],
        dst_ref=lower.at[blocks],
        send_sem=cell_sem.at[0],
        recv_sem=cell_sem.at[1],
        device_id=(before, core),
        device_id_type=MESH,
    )
    cell.start()
    every(1, blocks - 1, start_first)

    def push_product(js):
        products = []
        for j in js:
            push = push_ref[pl.ds(j, 1), :]
            high = push.astype(BF16)
            rest = push - high.astype(F32)
            middle = rest.astype(BF16)
            low = (rest - middle.astype(F32)).astype(BF16)
            rows = jnp.concatenate(
                [jnp.broadcast_to(part, (16, width)) for part in (high, middle, low)], axis=0
            )
            products.append(dot_nt(rows, inverse[j]))
        for j, product in zip(js, products):
            inverse_push[pl.ds(j, 1), :] = product[0:1] + product[16:17] + product[32:33]

    every(0, blocks, push_product)
    loads[5].wait()
    loads[6].wait()

    def inner(field, js):
        values = [field[js[0] - 1 + u] for u in range(len(js) + 2)]
        return [stiff(values[u], values[u + 1], values[u + 2], j) for u, j in enumerate(js)]

    def interior_first(js):
        finish_first(js, inner(x_round, js))

    for step in range(STEPS):
        if step > 0:
            e = 2 * step - 1
            every(1, blocks - 1, interior_first)
            known = ends_before(x_round)
            pairs = [ballast(x_ref[j], j) for j in (0, blocks - 1)]
            arrived(e)
            finish_first([0, blocks - 1], ends_after(e, x_round, known), pairs)
            post(e + 1, step_round[0], step_round[blocks - 1])
        e = 2 * step

        def interior_second(js):
            finish_second(js, inner(step_round, js), step == 0)

        every(1, blocks - 1, interior_second)
        known = ends_before(step_round)
        arrived(e)
        if step == 0:
            cell.wait()
            lower[0] = jnp.where(jnp.full((width, width), me, jnp.int32) > 0, lower[0].astype(F32), 0.0).astype(BF16)
            lower[blocks] = jnp.where(
                jnp.full((width, width), me, jnp.int32) < segments - 1, lower[blocks].astype(F32), 0.0
            ).astype(BF16)
        finish_second([0, blocks - 1], ends_after(e, step_round, known), step == 0)
        if step < STEPS - 1:
            post(e + 1, x_round[0], x_round[blocks - 1])

    weighted = jnp.sum(inverse_push[...] * sample_sum[...], axis=1, keepdims=True)
    pair[core] = jnp.sum(shape_ref[...].astype(F32) * weighted, axis=0, keepdims=True)

    def share_half(k, carry):
        pltpu.make_async_remote_copy(
            src_ref=pair.at[core],
            dst_ref=pair.at[core],
            send_sem=sum_sem.at[2],
            recv_sem=sum_sem.at[3],
            device_id=(me, lax.rem(core + k, halves)),
            device_id_type=MESH,
        ).start()
        return carry

    def share(k, carry):
        pltpu.make_async_remote_copy(
            src_ref=partials.at[me],
            dst_ref=partials.at[me],
            send_sem=sum_sem.at[0],
            recv_sem=sum_sem.at[1],
            device_id=(lax.rem(me + k, segments), core),
            device_id_type=MESH,
        ).start()
        return carry

    lax.fori_loop(1, halves, share_half, 0)
    result = pltpu.make_async_copy(x_ref, x_hbm, local_sem.at[7])
    result.start()
    other_half = pair.at[pl.ds(0, halves - 1)]
    pltpu.make_async_copy(other_half, other_half, sum_sem.at[3]).wait()
    partials[me] = jnp.sum(pair[...], axis=0)
    lax.fori_loop(1, segments, share, 0)
    for e in range(EXCHANGES):
        sent(e)
    pltpu.make_async_copy(other_half, other_half, sum_sem.at[2]).wait()
    result.wait()
    others = partials.at[pl.ds(0, segments - 1)]
    pltpu.make_async_copy(others, others, sum_sem.at[1]).wait()
    grad_ref[...] = jnp.sum(partials[...], axis=0)
    pltpu.make_async_copy(others, others, sum_sem.at[0]).wait()


def body(segments, halves, *arguments):
    (diag, lower, inverse, bed, regime, push, shapes, weights, table, joint) = arguments
    samples = weights.shape[0]
    blocks, width = diag.shape[0], diag.shape[1]
    terms = shapes.shape[1]
    vmem = pl.BlockSpec(memory_space=pltpu.VMEM)
    smem = pl.BlockSpec(memory_space=pltpu.SMEM)
    anywhere = pl.BlockSpec(memory_space=pltpu.HBM)
    field = (blocks, samples, width)
    rim = (EXCHANGES, samples, width)
    x, grad = pl.pallas_call(
        functools.partial(kernel, segments, halves),
        out_shape=(
            jax.ShapeDtypeStruct(field, F32),
            jax.ShapeDtypeStruct((1, terms), F32),
        ),
        in_specs=[anywhere, anywhere, anywhere, anywhere, smem, anywhere, anywhere, anywhere, smem, smem],
        out_specs=(anywhere, vmem),
        scratch_shapes=[
            pltpu.VMEM((blocks, width, width), BF16),
            pltpu.VMEM((blocks + 1, width, width), BF16),
            pltpu.VMEM((blocks, width, width), BF16),
            pltpu.VMEM(bed.shape, bed.dtype),
            pltpu.VMEM(push.shape, push.dtype),
            pltpu.VMEM(shapes.shape, shapes.dtype),
            pltpu.VMEM(weights.shape, weights.dtype),
            pltpu.VMEM(field, F32),
            pltpu.VMEM(field, F32),
            pltpu.VMEM(field, F32),
            pltpu.VMEM(field, F32),
            pltpu.VMEM(field, BF16),
            pltpu.VMEM(field, BF16),
            pltpu.VMEM((blocks, width), F32),
            pltpu.VMEM((blocks, width), F32),
            pltpu.VMEM(rim, BF16),
            pltpu.VMEM(rim, BF16),
            pltpu.VMEM((segments, 1, terms), F32),
            pltpu.VMEM((halves, 1, terms), F32),
            pltpu.VMEM(field, F32),
            pltpu.SemaphoreType.DMA((8,)),
            pltpu.SemaphoreType.DMA((EXCHANGES,)),
            pltpu.SemaphoreType.DMA((EXCHANGES,)),
            pltpu.SemaphoreType.DMA((EXCHANGES,)),
            pltpu.SemaphoreType.DMA((EXCHANGES,)),
            pltpu.SemaphoreType.DMA((2,)),
            pltpu.SemaphoreType.DMA((4,)),
        ]
        + [pltpu.VMEM((segments, samples, width), BF16)] * EXCHANGES,
        compiler_params=pltpu.CompilerParams(
            collective_id=0, has_side_effects=True, vmem_limit_bytes=63 * 1024 * 1024
        ),
    )(diag, lower, inverse, bed, regime, push, shapes, weights, table, joint)
    scale = math.sqrt(terms / (blocks * segments * samples * halves * width))
    return jnp.transpose(x, (1, 0, 2)), grad[0] * scale


def solution(mesh):
    placed = (
        P("seg", None, None),
        P("seg", None, None),
        P("seg", None, None),
        P("seg", None),
        P("seg"),
        P("seg", None),
        P("seg", None),
        P("samp", None),
        P("seg", None),
        P("seg", None),
    )
    return jax.shard_map(
        functools.partial(body, mesh.shape["seg"], mesh.shape["samp"]),
        mesh=mesh,
        in_specs=placed,
        out_specs=(P("samp", "seg", None), P()),
        check_vma=False,
    )
```

```python
import functools
import math

import jax
import jax.numpy as jnp
from jax import lax
from jax.experimental import pallas as pl
from jax.experimental.pallas import tpu as pltpu
from jax.sharding import PartitionSpec as P

STEPS = 4
EXCHANGES = 2 * STEPS - 1
GROUP = 10
F32 = jnp.float32
BF16 = jnp.bfloat16
MESH = pl.DeviceIdType.MESH


def dot_nt(left, right):
    return lax.dot_general(left, right, (((1,), (1,)), ((), ())), preferred_element_type=F32)


def dot_nn(left, right):
    return lax.dot_general(left, right, (((1,), (0,)), ((), ())), preferred_element_type=F32)


def kernel(
    segments,
    halves,
    diag_hbm,
    lower_hbm,
    inverse_hbm,
    bed_hbm,
    regime_ref,
    push_hbm,
    shape_hbm,
    weight_hbm,
    table_ref,
    joint_ref,
    x_hbm,
    grad_ref,
    diag,
    lower,
    inverse,
    bed_ref,
    push_ref,
    shape_ref,
    weight_ref,
    load,
    res,
    step_field,
    tangent,
    x_round,
    step_round,
    sample_sum,
    inverse_push,
    edge,
    below,
    partials,
    pair,
    x_ref,
    turned,
    local_sem,
    send_sem,
    recv_sem,
    edge_send,
    edge_recv,
    cell_sem,
    sum_sem,
    *gathered,
):
    blocks = diag.shape[0]
    samples, width = load.shape[1], load.shape[2]
    me = lax.axis_index("seg")
    core = lax.axis_index("samp")
    after = lax.rem(me + 1, segments)
    before = lax.rem(me + segments - 1, segments)
    peers = segments + halves - 2

    barrier = pltpu.get_barrier_semaphore()

    def greet(k, carry):
        pl.semaphore_signal(
            barrier, inc=1, device_id=(lax.rem(me + k, segments), core), device_id_type=MESH
        )
        return carry

    def greet_half(k, carry):
        pl.semaphore_signal(
            barrier, inc=1, device_id=(me, lax.rem(core + k, halves)), device_id_type=MESH
        )
        return carry

    loads = [
        pltpu.make_async_copy(weight_hbm, weight_ref, local_sem.at[3]),
        pltpu.make_async_copy(shape_hbm, shape_ref, local_sem.at[4]),
        pltpu.make_async_copy(push_hbm, push_ref, local_sem.at[5]),
        pltpu.make_async_copy(bed_hbm, bed_ref, local_sem.at[6]),
        pltpu.make_async_copy(
            inverse_hbm.at[pl.ds(1, blocks - 2)],
            inverse.at[pl.ds(1, blocks - 2)],
            local_sem.at[0],
        ),
        pltpu.make_async_copy(diag_hbm, diag, local_sem.at[1]),
        pltpu.make_async_copy(lower_hbm, lower.at[pl.ds(0, blocks)], local_sem.at[2]),
    ]
    end_loads = [
        pltpu.make_async_copy(inverse_hbm.at[j], inverse.at[j], local_sem.at[sem])
        for j, sem in ((0, 8), (blocks - 1, 9))
    ]
    for copy in loads[:3] + end_loads + loads[3:]:
        copy.start()
    lax.fori_loop(1, segments, greet, 0)
    lax.fori_loop(1, halves, greet_half, 0)
    for copy in loads[:3]:
        copy.wait()

    temperature = dot_nt(weight_ref[...], shape_ref[...])

    def set_load(j):
        load[j] = temperature[:, j : j + 1] * push_ref[j : j + 1, :]

    set_load(0)
    set_load(blocks - 1)
    sample_sum[...] = jnp.zeros_like(sample_sum)

    def partner(k):
        return me ^ k if segments & (segments - 1) == 0 else lax.rem(me + k, segments)

    def post(e, first_value, last_value):
        gathered[e][me] = first_value
        edge[e] = last_value

        def send(k, carry):
            pltpu.make_async_remote_copy(
                src_ref=gathered[e].at[me],
                dst_ref=gathered[e].at[me],
                send_sem=send_sem.at[e],
                recv_sem=recv_sem.at[e],
                device_id=(partner(segments - k), core),
                device_id_type=MESH,
            ).start()
            return carry

        pltpu.make_async_remote_copy(
            src_ref=edge.at[e],
            dst_ref=below.at[e],
            send_sem=edge_send.at[e],
            recv_sem=edge_recv.at[e],
            device_id=(after, core),
            device_id_type=MESH,
        ).start()
        lax.fori_loop(1, segments, send, 0)

    def arrived(e):
        others = gathered[e].at[pl.ds(0, segments - 1)]
        pltpu.make_async_copy(others, others, recv_sem.at[e]).wait()
        pltpu.make_async_copy(below.at[e], below.at[e], edge_recv.at[e]).wait()

    def sent(e):
        others = gathered[e].at[pl.ds(0, segments - 1)]
        pltpu.make_async_copy(others, others, send_sem.at[e]).wait()
        pltpu.make_async_copy(edge.at[e], edge.at[e], edge_send.at[e]).wait()

    def stiff(low, own, high, j):
        pair = jnp.concatenate([low, own], axis=1)
        cells = jnp.concatenate([lower[j], diag[j]], axis=1)
        return dot_nt(pair, cells) + dot_nn(high, lower[j + 1])

    def spring(e, own):
        own = own.astype(F32)
        total = jnp.zeros_like(own)
        for l in range(table_ref.shape[1]):
            partner = gathered[e][table_ref[0, l]].astype(F32)
            total = total + joint_ref[0, l] * (own - partner)
        return total

    def ends_before(field):
        low = dot_nt(field[0], diag[0]) + dot_nn(field[1], lower[1])
        pair_cells = jnp.concatenate([lower[blocks - 1], diag[blocks - 1]], axis=1)
        high = dot_nt(jnp.concatenate([field[blocks - 2], field[blocks - 1]], axis=1), pair_cells)
        return low, high

    def ends_after(e, field, known):
        low = known[0] + dot_nn(below[e], turned[2]) + spring(e, field[0])
        high = known[1] + dot_nn(gathered[e][after], lower[blocks])
        return [low, high]

    def ballast(x, j):
        k = bed_ref[pl.ds(j, 1), :]
        code = jnp.full(x.shape, regime_ref[j], jnp.int32)
        fraction = 1.0 / (1.0 + jnp.abs(x))
        slide = jnp.tanh(x)
        unit = jnp.where(code == 0, x, jnp.where(code == 1, x * fraction, slide))
        slope = jnp.where(
            code == 0, 1.0, jnp.where(code == 1, fraction * fraction, 1.0 - slide * slide)
        )
        return k * unit, k * slope

    def precondition(j, value):
        value = value.astype(BF16)
        if isinstance(j, int) and j in (0, blocks - 1):
            return dot_nn(value, turned[0 if j == 0 else 1])
        return dot_nt(value, inverse[j])

    def finish_first(js, kxs, pairs=None):
        if pairs is None:
            pairs = [ballast(x_ref[j], j) for j in js]
        residuals = [load[j] - kx - pair[0] for j, kx, pair in zip(js, kxs, pairs)]
        firsts = [precondition(j, residual) for j, residual in zip(js, residuals)]
        for j, residual, pair, first in zip(js, residuals, pairs, firsts):
            res[j] = residual
            tangent[j] = pair[1]
            step_field[j] = first
            step_round[j] = first.astype(BF16)

    def finish_second(js, kfs, start):
        firsts = [step_field[j] for j in js]
        if start:
            seconds = [
                load[j] - kf - bed_ref[pl.ds(j, 1), :] * first
                for j, kf, first in zip(js, kfs, firsts)
            ]
            xs = firsts
        else:
            seconds = [
                res[j] - kf - tangent[j] * first for j, kf, first in zip(js, kfs, firsts)
            ]
            xs = [x_ref[j] + first for j, first in zip(js, firsts)]
        xs = [x + precondition(j, second) for j, x, second in zip(js, xs, seconds)]
        rounds = [x.astype(BF16) for x in xs]
        sums = [jnp.sum(rounded.astype(F32), axis=0, keepdims=True) for rounded in rounds]
        for j, x, rounded, total in zip(js, xs, rounds, sums):
            x_ref[j] = x
            x_round[j] = rounded
            sample_sum[pl.ds(j, 1), :] += total

    def every(start, stop, work):
        count = (stop - start) // GROUP

        def group(i, carry):
            work([start + i * GROUP + u for u in range(GROUP)])
            return carry

        lax.fori_loop(0, count, group, 0)
        if start + count * GROUP < stop:
            work(list(range(start + count * GROUP, stop)))

    def start_first(js):
        firsts = [dot_nt(load[j].astype(BF16), inverse[j]) for j in js]
        for j, first in zip(js, firsts):
            step_field[j] = first
            step_round[j] = first.astype(BF16)

    for copy in end_loads:
        copy.wait()
    start_first([0, blocks - 1])
    pl.semaphore_wait(barrier, peers)
    post(0, step_round[0], step_round[blocks - 1])
    cell = pltpu.make_async_remote_copy(
        src_ref=lower_hbm.at[0],
        dst_ref=lower.at[blocks],
        send_sem=cell_sem.at[0],
        recv_sem=cell_sem.at[1],
        device_id=(before, core),
        device_id_type=MESH,
    )
    cell.start()
    for j in range(1, blocks - 1):
        set_load(j)
    loads[3].wait()
    loads[4].wait()
    every(1, blocks - 1, start_first)

    def push_product(js):
        products = []
        for j in js:
            push = push_ref[pl.ds(j, 1), :]
            high = push.astype(BF16)
            rest = push - high.astype(F32)
            middle = rest.astype(BF16)
            low = (rest - middle.astype(F32)).astype(BF16)
            rows = jnp.concatenate(
                [jnp.broadcast_to(part, (16, width)) for part in (high, middle, low)], axis=0
            )
            products.append(dot_nt(rows, inverse[j]))
        for j, product in zip(js, products):
            inverse_push[pl.ds(j, 1), :] = product[0:1] + product[16:17] + product[32:33]

    every(0, blocks, push_product)
    loads[5].wait()
    loads[6].wait()
    turned[0] = inverse[0].astype(F32).T.astype(BF16)
    turned[1] = inverse[blocks - 1].astype(F32).T.astype(BF16)
    has_before = jnp.full((width, width), me, jnp.int32) > 0
    turned[2] = jnp.where(has_before, lower[0].astype(F32).T, 0.0).astype(BF16)

    def inner(field, js):
        values = [field[js[0] - 1 + u] for u in range(len(js) + 2)]
        return [stiff(values[u], values[u + 1], values[u + 2], j) for u, j in enumerate(js)]

    def interior_first(js):
        finish_first(js, inner(x_round, js))

    for step in range(STEPS):
        if step > 0:
            e = 2 * step - 1
            every(1, blocks - 1, interior_first)
            known = ends_before(x_round)
            pairs = [ballast(x_ref[j], j) for j in (0, blocks - 1)]
            arrived(e)
            finish_first([0, blocks - 1], ends_after(e, x_round, known), pairs)
            post(e + 1, step_round[0], step_round[blocks - 1])
        e = 2 * step

        def interior_second(js):
            finish_second(js, inner(step_round, js), step == 0)

        every(1, blocks - 1, interior_second)
        known = ends_before(step_round)
        arrived(e)
        if step == 0:
            cell.wait()
            lower[blocks] = jnp.where(
                jnp.full((width, width), me, jnp.int32) < segments - 1, lower[blocks].astype(F32), 0.0
            ).astype(BF16)
        finish_second([0, blocks - 1], ends_after(e, step_round, known), step == 0)
        if step < STEPS - 1:
            post(e + 1, x_round[0], x_round[blocks - 1])

    weighted = jnp.sum(inverse_push[...] * sample_sum[...], axis=1, keepdims=True)
    pair[core] = jnp.sum(shape_ref[...].astype(F32) * weighted, axis=0, keepdims=True)

    def share_half(k, carry):
        pltpu.make_async_remote_copy(
            src_ref=pair.at[core],
            dst_ref=pair.at[core],
            send_sem=sum_sem.at[2],
            recv_sem=sum_sem.at[3],
            device_id=(me, lax.rem(core + k, halves)),
            device_id_type=MESH,
        ).start()
        return carry

    def share(k, carry):
        pltpu.make_async_remote_copy(
            src_ref=partials.at[me],
            dst_ref=partials.at[me],
            send_sem=sum_sem.at[0],
            recv_sem=sum_sem.at[1],
            device_id=(lax.rem(me + k, segments), core),
            device_id_type=MESH,
        ).start()
        return carry

    lax.fori_loop(1, halves, share_half, 0)
    result = pltpu.make_async_copy(x_ref, x_hbm, local_sem.at[7])
    result.start()
    other_half = pair.at[pl.ds(0, halves - 1)]
    pltpu.make_async_copy(other_half, other_half, sum_sem.at[3]).wait()
    partials[me] = jnp.sum(pair[...], axis=0)
    lax.fori_loop(1, segments, share, 0)
    for e in range(EXCHANGES):
        sent(e)
    pltpu.make_async_copy(other_half, other_half, sum_sem.at[2]).wait()
    result.wait()
    others = partials.at[pl.ds(0, segments - 1)]
    pltpu.make_async_copy(others, others, sum_sem.at[1]).wait()
    grad_ref[...] = jnp.sum(partials[...], axis=0)
    pltpu.make_async_copy(others, others, sum_sem.at[0]).wait()


def body(segments, halves, *arguments):
    (diag, lower, inverse, bed, regime, push, shapes, weights, table, joint) = arguments
    samples = weights.shape[0]
    blocks, width = diag.shape[0], diag.shape[1]
    terms = shapes.shape[1]
    vmem = pl.BlockSpec(memory_space=pltpu.VMEM)
    smem = pl.BlockSpec(memory_space=pltpu.SMEM)
    anywhere = pl.BlockSpec(memory_space=pltpu.HBM)
    field = (blocks, samples, width)
    rim = (EXCHANGES, samples, width)
    x, grad = pl.pallas_call(
        functools.partial(kernel, segments, halves),
        out_shape=(
            jax.ShapeDtypeStruct(field, F32),
            jax.ShapeDtypeStruct((1, terms), F32),
        ),
        in_specs=[anywhere, anywhere, anywhere, anywhere, smem, anywhere, anywhere, anywhere, smem, smem],
        out_specs=(anywhere, vmem),
        scratch_shapes=[
            pltpu.VMEM((blocks, width, width), BF16),
            pltpu.VMEM((blocks + 1, width, width), BF16),
            pltpu.VMEM((blocks, width, width), BF16),
            pltpu.VMEM(bed.shape, bed.dtype),
            pltpu.VMEM(push.shape, push.dtype),
            pltpu.VMEM(shapes.shape, shapes.dtype),
            pltpu.VMEM(weights.shape, weights.dtype),
            pltpu.VMEM(field, F32),
            pltpu.VMEM(field, F32),
            pltpu.VMEM(field, F32),
            pltpu.VMEM(field, F32),
            pltpu.VMEM(field, BF16),
            pltpu.VMEM(field, BF16),
            pltpu.VMEM((blocks, width), F32),
            pltpu.VMEM((blocks, width), F32),
            pltpu.VMEM(rim, BF16),
            pltpu.VMEM(rim, BF16),
            pltpu.VMEM((segments, 1, terms), F32),
            pltpu.VMEM((halves, 1, terms), F32),
            pltpu.VMEM(field, F32),
            pltpu.VMEM((3, width, width), BF16),
            pltpu.SemaphoreType.DMA((10,)),
            pltpu.SemaphoreType.DMA((EXCHANGES,)),
            pltpu.SemaphoreType.DMA((EXCHANGES,)),
            pltpu.SemaphoreType.DMA((EXCHANGES,)),
            pltpu.SemaphoreType.DMA((EXCHANGES,)),
            pltpu.SemaphoreType.DMA((2,)),
            pltpu.SemaphoreType.DMA((4,)),
        ]
        + [pltpu.VMEM((segments, samples, width), BF16)] * EXCHANGES,
        compiler_params=pltpu.CompilerParams(
            collective_id=0, has_side_effects=True, vmem_limit_bytes=63 * 1024 * 1024
        ),
    )(diag, lower, inverse, bed, regime, push, shapes, weights, table, joint)
    scale = math.sqrt(terms / (blocks * segments * samples * halves * width))
    return jnp.transpose(x, (1, 0, 2)), grad[0] * scale


def solution(mesh):
    placed = (
        P("seg", None, None),
        P("seg", None, None),
        P("seg", None, None),
        P("seg", None),
        P("seg"),
        P("seg", None),
        P("seg", None),
        P("samp", None),
        P("seg", None),
        P("seg", None),
    )
    return jax.shard_map(
        functools.partial(body, mesh.shape["seg"], mesh.shape["samp"]),
        mesh=mesh,
        in_specs=placed,
        out_specs=(P("samp", "seg", None), P()),
        check_vma=False,
    )
```

```python
import functools
import math

import jax
import jax.numpy as jnp
from jax import lax
from jax.experimental import pallas as pl
from jax.experimental.pallas import tpu as pltpu
from jax.sharding import PartitionSpec as P

STEPS = 4
EXCHANGES = 2 * STEPS - 1
GROUP = 10
F32 = jnp.float32
BF16 = jnp.bfloat16
MESH = pl.DeviceIdType.MESH


def dot_nt(left, right):
    return lax.dot_general(left, right, (((1,), (1,)), ((), ())), preferred_element_type=F32)


def dot_nn(left, right):
    return lax.dot_general(left, right, (((1,), (0,)), ((), ())), preferred_element_type=F32)


def kernel(
    segments,
    halves,
    diag_hbm,
    lower_hbm,
    inverse_hbm,
    bed_hbm,
    regime_ref,
    push_hbm,
    shape_hbm,
    weight_hbm,
    table_ref,
    joint_ref,
    x_hbm,
    grad_ref,
    diag,
    lower,
    inverse,
    bed_ref,
    push_ref,
    shape_ref,
    weight_ref,
    load,
    res,
    step_field,
    tangent,
    x_round,
    step_round,
    sample_sum,
    inverse_push,
    edge,
    below,
    partials,
    pair,
    x_ref,
    turned,
    local_sem,
    send_sem,
    recv_sem,
    edge_send,
    edge_recv,
    cell_sem,
    sum_sem,
    *gathered,
):
    blocks = diag.shape[0]
    samples, width = load.shape[1], load.shape[2]
    me = lax.axis_index("seg")
    core = lax.axis_index("samp")
    after = lax.rem(me + 1, segments)
    before = lax.rem(me + segments - 1, segments)
    peers = segments + halves - 2

    barrier = pltpu.get_barrier_semaphore()

    def greet(k, carry):
        pl.semaphore_signal(
            barrier, inc=1, device_id=(lax.rem(me + k, segments), core), device_id_type=MESH
        )
        return carry

    def greet_half(k, carry):
        pl.semaphore_signal(
            barrier, inc=1, device_id=(me, lax.rem(core + k, halves)), device_id_type=MESH
        )
        return carry

    loads = [
        pltpu.make_async_copy(weight_hbm, weight_ref, local_sem.at[3]),
        pltpu.make_async_copy(shape_hbm, shape_ref, local_sem.at[4]),
        pltpu.make_async_copy(push_hbm, push_ref, local_sem.at[5]),
        pltpu.make_async_copy(bed_hbm, bed_ref, local_sem.at[6]),
        pltpu.make_async_copy(
            inverse_hbm.at[pl.ds(1, blocks - 2)],
            inverse.at[pl.ds(1, blocks - 2)],
            local_sem.at[0],
        ),
        pltpu.make_async_copy(diag_hbm, diag, local_sem.at[1]),
        pltpu.make_async_copy(lower_hbm, lower.at[pl.ds(0, blocks)], local_sem.at[2]),
    ]
    end_loads = [
        pltpu.make_async_copy(inverse_hbm.at[j], inverse.at[j], local_sem.at[sem])
        for j, sem in ((0, 8), (blocks - 1, 9))
    ]
    for copy in loads[:3] + end_loads + loads[3:]:
        copy.start()
    lax.fori_loop(1, segments, greet, 0)
    lax.fori_loop(1, halves, greet_half, 0)
    for copy in loads[:3]:
        copy.wait()

    temperature = dot_nt(weight_ref[...], shape_ref[...])

    def set_load(j):
        load[j] = temperature[:, j : j + 1] * push_ref[j : j + 1, :]

    set_load(0)
    set_load(blocks - 1)
    sample_sum[...] = jnp.zeros_like(sample_sum)

    def partner(k):
        return me ^ k if segments & (segments - 1) == 0 else lax.rem(me + k, segments)

    def mask(k):
        if segments % 4:
            return k
        half, quarter = segments // 2, segments // 4
        crossed = segments - 1 - (k - 1) // 2 - lax.rem(k - 1, 2) * quarter
        return jnp.where(k <= half, crossed, segments - k)

    def post(e, first_value, last_value):
        gathered[e][me] = first_value
        edge[e] = last_value

        def send(k, carry):
            pltpu.make_async_remote_copy(
                src_ref=gathered[e].at[me],
                dst_ref=gathered[e].at[me],
                send_sem=send_sem.at[e],
                recv_sem=recv_sem.at[e],
                device_id=(partner(mask(k)), core),
                device_id_type=MESH,
            ).start()
            return carry

        pltpu.make_async_remote_copy(
            src_ref=edge.at[e],
            dst_ref=below.at[e],
            send_sem=edge_send.at[e],
            recv_sem=edge_recv.at[e],
            device_id=(after, core),
            device_id_type=MESH,
        ).start()
        lax.fori_loop(1, segments, send, 0)

    def arrived(e):
        others = gathered[e].at[pl.ds(0, segments - 1)]
        pltpu.make_async_copy(others, others, recv_sem.at[e]).wait()
        pltpu.make_async_copy(below.at[e], below.at[e], edge_recv.at[e]).wait()

    def sent(e):
        others = gathered[e].at[pl.ds(0, segments - 1)]
        pltpu.make_async_copy(others, others, send_sem.at[e]).wait()
        pltpu.make_async_copy(edge.at[e], edge.at[e], edge_send.at[e]).wait()

    def stiff(low, own, high, j):
        pair = jnp.concatenate([low, own], axis=1)
        cells = jnp.concatenate([lower[j], diag[j]], axis=1)
        return dot_nt(pair, cells) + dot_nn(high, lower[j + 1])

    def spring(e, own):
        own = own.astype(F32)
        total = jnp.zeros_like(own)
        for l in range(table_ref.shape[1]):
            partner = gathered[e][table_ref[0, l]].astype(F32)
            total = total + joint_ref[0, l] * (own - partner)
        return total

    def ends_before(field):
        low = dot_nt(field[0], diag[0]) + dot_nn(field[1], lower[1])
        pair_cells = jnp.concatenate([lower[blocks - 1], diag[blocks - 1]], axis=1)
        high = dot_nt(jnp.concatenate([field[blocks - 2], field[blocks - 1]], axis=1), pair_cells)
        return low, high

    def ends_after(e, field, known):
        low = known[0] + dot_nn(below[e], turned[2]) + spring(e, field[0])
        high = known[1] + dot_nn(gathered[e][after], lower[blocks])
        return [low, high]

    def ballast(x, j):
        k = bed_ref[pl.ds(j, 1), :]
        code = jnp.full(x.shape, regime_ref[j], jnp.int32)
        fraction = 1.0 / (1.0 + jnp.abs(x))
        slide = jnp.tanh(x)
        unit = jnp.where(code == 0, x, jnp.where(code == 1, x * fraction, slide))
        slope = jnp.where(
            code == 0, 1.0, jnp.where(code == 1, fraction * fraction, 1.0 - slide * slide)
        )
        return k * unit, k * slope

    def precondition(j, value):
        value = value.astype(BF16)
        if isinstance(j, int) and j in (0, blocks - 1):
            return dot_nn(value, turned[0 if j == 0 else 1])
        return dot_nt(value, inverse[j])

    def finish_first(js, kxs, pairs=None):
        if pairs is None:
            pairs = [ballast(x_ref[j], j) for j in js]
        residuals = [load[j] - kx - pair[0] for j, kx, pair in zip(js, kxs, pairs)]
        firsts = [precondition(j, residual) for j, residual in zip(js, residuals)]
        for j, residual, pair, first in zip(js, residuals, pairs, firsts):
            res[j] = residual
            tangent[j] = pair[1]
            step_field[j] = first
            step_round[j] = first.astype(BF16)

    def finish_second(js, kfs, start):
        firsts = [step_field[j] for j in js]
        if start:
            seconds = [
                load[j] - kf - bed_ref[pl.ds(j, 1), :] * first
                for j, kf, first in zip(js, kfs, firsts)
            ]
            xs = firsts
        else:
            seconds = [
                res[j] - kf - tangent[j] * first for j, kf, first in zip(js, kfs, firsts)
            ]
            xs = [x_ref[j] + first for j, first in zip(js, firsts)]
        xs = [x + precondition(j, second) for j, x, second in zip(js, xs, seconds)]
        rounds = [x.astype(BF16) for x in xs]
        sums = [jnp.sum(rounded.astype(F32), axis=0, keepdims=True) for rounded in rounds]
        for j, x, rounded, total in zip(js, xs, rounds, sums):
            x_ref[j] = x
            x_round[j] = rounded
            sample_sum[pl.ds(j, 1), :] += total

    def every(start, stop, work):
        count = (stop - start) // GROUP

        def group(i, carry):
            work([start + i * GROUP + u for u in range(GROUP)])
            return carry

        lax.fori_loop(0, count, group, 0)
        if start + count * GROUP < stop:
            work(list(range(start + count * GROUP, stop)))

    def start_first(js):
        firsts = [dot_nt(load[j].astype(BF16), inverse[j]) for j in js]
        for j, first in zip(js, firsts):
            step_field[j] = first
            step_round[j] = first.astype(BF16)

    for copy in end_loads:
        copy.wait()
    start_first([0, blocks - 1])
    pl.semaphore_wait(barrier, peers)
    post(0, step_round[0], step_round[blocks - 1])
    cell = pltpu.make_async_remote_copy(
        src_ref=lower_hbm.at[0],
        dst_ref=lower.at[blocks],
        send_sem=cell_sem.at[0],
        recv_sem=cell_sem.at[1],
        device_id=(before, core),
        device_id_type=MESH,
    )
    cell.start()
    for j in range(1, blocks - 1):
        set_load(j)
    loads[3].wait()
    loads[4].wait()
    every(1, blocks - 1, start_first)

    def push_product(js):
        products = []
        for j in js:
            push = push_ref[pl.ds(j, 1), :]
            high = push.astype(BF16)
            rest = push - high.astype(F32)
            middle = rest.astype(BF16)
            low = (rest - middle.astype(F32)).astype(BF16)
            rows = jnp.concatenate(
                [jnp.broadcast_to(part, (16, width)) for part in (high, middle, low)], axis=0
            )
            products.append(dot_nt(rows, inverse[j]))
        for j, product in zip(js, products):
            inverse_push[pl.ds(j, 1), :] = product[0:1] + product[16:17] + product[32:33]

    every(0, blocks, push_product)
    loads[5].wait()
    loads[6].wait()
    turned[0] = inverse[0].astype(F32).T.astype(BF16)
    turned[1] = inverse[blocks - 1].astype(F32).T.astype(BF16)
    has_before = jnp.full((width, width), me, jnp.int32) > 0
    turned[2] = jnp.where(has_before, lower[0].astype(F32).T, 0.0).astype(BF16)

    def inner(field, js):
        values = [field[js[0] - 1 + u] for u in range(len(js) + 2)]
        return [stiff(values[u], values[u + 1], values[u + 2], j) for u, j in enumerate(js)]

    def interior_first(js):
        finish_first(js, inner(x_round, js))

    for step in range(STEPS):
        if step > 0:
            e = 2 * step - 1
            every(1, blocks - 1, interior_first)
            known = ends_before(x_round)
            pairs = [ballast(x_ref[j], j) for j in (0, blocks - 1)]
            arrived(e)
            finish_first([0, blocks - 1], ends_after(e, x_round, known), pairs)
            post(e + 1, step_round[0], step_round[blocks - 1])
        e = 2 * step

        def interior_second(js):
            finish_second(js, inner(step_round, js), step == 0)

        every(1, blocks - 1, interior_second)
        known = ends_before(step_round)
        arrived(e)
        if step == 0:
            cell.wait()
            lower[blocks] = jnp.where(
                jnp.full((width, width), me, jnp.int32) < segments - 1, lower[blocks].astype(F32), 0.0
            ).astype(BF16)
        finish_second([0, blocks - 1], ends_after(e, step_round, known), step == 0)
        if step < STEPS - 1:
            post(e + 1, x_round[0], x_round[blocks - 1])

    weighted = jnp.sum(inverse_push[...] * sample_sum[...], axis=1, keepdims=True)
    pair[core] = jnp.sum(shape_ref[...].astype(F32) * weighted, axis=0, keepdims=True)

    def share_half(k, carry):
        pltpu.make_async_remote_copy(
            src_ref=pair.at[core],
            dst_ref=pair.at[core],
            send_sem=sum_sem.at[2],
            recv_sem=sum_sem.at[3],
            device_id=(me, lax.rem(core + k, halves)),
            device_id_type=MESH,
        ).start()
        return carry

    def share(k, carry):
        pltpu.make_async_remote_copy(
            src_ref=partials.at[me],
            dst_ref=partials.at[me],
            send_sem=sum_sem.at[0],
            recv_sem=sum_sem.at[1],
            device_id=(lax.rem(me + k, segments), core),
            device_id_type=MESH,
        ).start()
        return carry

    lax.fori_loop(1, halves, share_half, 0)
    result = pltpu.make_async_copy(x_ref, x_hbm, local_sem.at[7])
    result.start()
    other_half = pair.at[pl.ds(0, halves - 1)]
    pltpu.make_async_copy(other_half, other_half, sum_sem.at[3]).wait()
    partials[me] = jnp.sum(pair[...], axis=0)
    lax.fori_loop(1, segments, share, 0)
    for e in range(EXCHANGES):
        sent(e)
    pltpu.make_async_copy(other_half, other_half, sum_sem.at[2]).wait()
    result.wait()
    others = partials.at[pl.ds(0, segments - 1)]
    pltpu.make_async_copy(others, others, sum_sem.at[1]).wait()
    grad_ref[...] = jnp.sum(partials[...], axis=0)
    pltpu.make_async_copy(others, others, sum_sem.at[0]).wait()


def body(segments, halves, *arguments):
    (diag, lower, inverse, bed, regime, push, shapes, weights, table, joint) = arguments
    samples = weights.shape[0]
    blocks, width = diag.shape[0], diag.shape[1]
    terms = shapes.shape[1]
    vmem = pl.BlockSpec(memory_space=pltpu.VMEM)
    smem = pl.BlockSpec(memory_space=pltpu.SMEM)
    anywhere = pl.BlockSpec(memory_space=pltpu.HBM)
    field = (blocks, samples, width)
    rim = (EXCHANGES, samples, width)
    x, grad = pl.pallas_call(
        functools.partial(kernel, segments, halves),
        out_shape=(
            jax.ShapeDtypeStruct(field, F32),
            jax.ShapeDtypeStruct((1, terms), F32),
        ),
        in_specs=[anywhere, anywhere, anywhere, anywhere, smem, anywhere, anywhere, anywhere, smem, smem],
        out_specs=(anywhere, vmem),
        scratch_shapes=[
            pltpu.VMEM((blocks, width, width), BF16),
            pltpu.VMEM((blocks + 1, width, width), BF16),
            pltpu.VMEM((blocks, width, width), BF16),
            pltpu.VMEM(bed.shape, bed.dtype),
            pltpu.VMEM(push.shape, push.dtype),
            pltpu.VMEM(shapes.shape, shapes.dtype),
            pltpu.VMEM(weights.shape, weights.dtype),
            pltpu.VMEM(field, F32),
            pltpu.VMEM(field, F32),
            pltpu.VMEM(field, F32),
            pltpu.VMEM(field, F32),
            pltpu.VMEM(field, BF16),
            pltpu.VMEM(field, BF16),
            pltpu.VMEM((blocks, width), F32),
            pltpu.VMEM((blocks, width), F32),
            pltpu.VMEM(rim, BF16),
            pltpu.VMEM(rim, BF16),
            pltpu.VMEM((segments, 1, terms), F32),
            pltpu.VMEM((halves, 1, terms), F32),
            pltpu.VMEM(field, F32),
            pltpu.VMEM((3, width, width), BF16),
            pltpu.SemaphoreType.DMA((10,)),
            pltpu.SemaphoreType.DMA((EXCHANGES,)),
            pltpu.SemaphoreType.DMA((EXCHANGES,)),
            pltpu.SemaphoreType.DMA((EXCHANGES,)),
            pltpu.SemaphoreType.DMA((EXCHANGES,)),
            pltpu.SemaphoreType.DMA((2,)),
            pltpu.SemaphoreType.DMA((4,)),
        ]
        + [pltpu.VMEM((segments, samples, width), BF16)] * EXCHANGES,
        compiler_params=pltpu.CompilerParams(
            collective_id=0, has_side_effects=True, vmem_limit_bytes=63 * 1024 * 1024
        ),
    )(diag, lower, inverse, bed, regime, push, shapes, weights, table, joint)
    scale = math.sqrt(terms / (blocks * segments * samples * halves * width))
    return jnp.transpose(x, (1, 0, 2)), grad[0] * scale


def solution(mesh):
    placed = (
        P("seg", None, None),
        P("seg", None, None),
        P("seg", None, None),
        P("seg", None),
        P("seg"),
        P("seg", None),
        P("seg", None),
        P("samp", None),
        P("seg", None),
        P("seg", None),
    )
    return jax.shard_map(
        functools.partial(body, mesh.shape["seg"], mesh.shape["samp"]),
        mesh=mesh,
        in_specs=placed,
        out_specs=(P("samp", "seg", None), P()),
        check_vma=False,
    )
```
